32 devices in a mesh: exp: 8 (over y, x, core), seq: 4 (over z).
Axes of the slice: x: 2, y: 2, z: 4, core: 2. Of those that a mesh axis runs over, the one named last changes fastest.
Arguments:
- queries: bfloat16 [4096, 2048], P(('exp', 'seq')), may hold values from -400 to 400
- keys: bfloat16 [4096, 256], P(('exp', 'seq')), may hold values from -5 to 5
- values: bfloat16 [4096, 256], P(('exp', 'seq')), may hold values from -6 to 6
- resid: bfloat16 [4096, 2048], P(('exp', 'seq')), may hold values from -50 to 50
- seg_ids: int32 [4096], P('exp'), may hold values from 0 to 63, never falling along the last dimension, each value on 1 to 256 neighbouring positions
- norm_gain: float32 [2048], replicated, may hold values from 0.1 to 1.9
- expert_ids: int32 [4096], P(('exp', 'seq')), may hold values from 0 to 31, as said below
- gate_weights: float32 [4096], P(('exp', 'seq')), may hold values from 0.1 to 0.9
- w_in: bfloat16 [32, 2048, 1536], P(('exp', 'seq')), may hold values from -0.125 to 0.125
- w_out: bfloat16 [32, 768, 2048], P(('exp', 'seq')), may hold values from -0.21875 to 0.21875
Outputs:
- output: bfloat16 [4096, 2048], P(('exp', 'seq'))
The draws below stay inside these ranges and needn't reach their ends.
Inputs may be any that keep to these rules, and one draw needn't show every extreme that they name: `expert_ids`: within each aligned block of 128 tokens (the tokens of one device) no expert is named more than 8 times, and the bound is reached.
All inputs are finite; a program needn't handle non-finite values.
Results may differ from the reference program's by a relative error of at most 0.0055.
Values may be sent and summed in bfloat16 or wider, within the bound.
No kernel may reach another device: no remote copies, remote signals or barrier semaphores. Data moves between devices by JAX's collectives and lax.ppermute only.
A program may use at most 64 MiB of HBM per device.

```python
import math
import jax
import jax.numpy as jnp
import numpy as np
from jax import lax

D = 2048
HD = 128
HEADS = 16
KVH = 2
FF = 768
TOK_DEV = 128
LEN = 512
TOKENS = 4096
EXPERTS = 32
SPLITS = 1
FFS = 768
SLOT_CAP = 8
HEAD_GROUP = 8
DOCS = 64
N_EXP = 8
N_SEQ = 4


def shared_keys(key):
    drawn_key = jax.random.fold_in(key, 12)
    normal_draw = jnp.clip(jax.random.normal(drawn_key, (TOKENS, KVH * HD), jnp.float32), -4.5, 4.5)
    return normal_draw


def draw_keys(key, part):
    normal_draw = shared_keys(key)
    return normal_draw.astype(jnp.bfloat16)


def draw_queries(key, part):
    own_key = jax.random.fold_in(key, 3)
    query_draw = jnp.clip(jax.random.normal(own_key, (TOKENS, HEADS * HD), jnp.float32), -5.0, 5.0)
    return query_draw.astype(jnp.bfloat16)


def draw_resid(key, part):
    own_key = jax.random.fold_in(key, 7)
    noise_key = jax.random.fold_in(own_key, 0)
    normal_draw = jnp.clip(jax.random.normal(noise_key, (TOKENS, D), jnp.float32), -5.0, 5.0)
    return normal_draw.astype(jnp.bfloat16)


def draw_expert_ids(key, part):
    own_key = jax.random.fold_in(key, 9)
    hot_key, rank_key, score_key, order_key = jax.random.split(own_key, 4)
    blocks = TOKENS // TOK_DEV
    slot_count = EXPERTS * SLOT_CAP
    hottest = jax.random.randint(hot_key, (), 0, EXPERTS)
    ranking = jax.random.permutation(rank_key, EXPERTS)
    slot_expert = jnp.arange(slot_count) // SLOT_CAP
    favour = (EXPERTS - ranking[slot_expert]) * 4096 // EXPERTS
    scores = jax.random.randint(score_key, (blocks, slot_count), 0, 4096) + favour[None, :]
    scores = jnp.where(slot_expert[None, :] == hottest, 16384, scores)
    scores = scores * slot_count + jnp.arange(slot_count)[None, :]
    chosen = lax.top_k(scores, TOK_DEV)[1]
    picked = chosen // SLOT_CAP
    shuffle_keys = jax.random.randint(order_key, (blocks, TOK_DEV), 0, 1 << 20) * TOK_DEV + jnp.arange(TOK_DEV)[None, :]
    shuffle = jnp.argsort(shuffle_keys, axis=1, stable=True)
    return jnp.take_along_axis(picked, shuffle, axis=1).reshape(TOKENS).astype(jnp.int32)


def level_of(key, extent, cuts, smallest, largest):
    gain = 1.0
    for dim, parts in cuts:
        heights = jax.random.uniform(jax.random.fold_in(jax.random.fold_in(key, 6), dim), (parts,), jnp.float32, smallest / len(cuts), largest / len(cuts))
        gain = gain * jnp.repeat(jnp.exp(heights), extent[dim] // parts).reshape((-1,) + (1,) * (len(extent) - 1 - dim))
    return gain


def split_up(count, total, reach, slope):
    weights = [(1 << 20) // math.isqrt(grade ** slope) + 1 for grade in range(2, count + 1)]
    surplus, counts = total - reach - (count - 1), [1] * (count - 1)
    while surplus > 0:
        candidates = [i for i in range(count - 1) if counts[i] < reach]
        mass, left = sum([weights[i] for i in candidates]), surplus
        for i in candidates:
            addition = min(reach - counts[i], max(1, left * weights[i] // mass), surplus)
            counts[i] = counts[i] + addition
            surplus = surplus - addition
    return np.array([reach] + counts)


def uneven(rng, count, total, bound, slope):
    if count == 2:
        one = jax.random.randint(rng, (), max(1, total - bound), min(bound, total - 1) + 1)
        return jnp.stack([one, total - one])
    lengths = jnp.asarray(split_up(count, total, bound, slope), jnp.int32)
    pairs = (count - 1) // 2
    donor, receiver = lengths[1:1 + 2 * pairs:2], lengths[2:2 + 2 * pairs:2]
    room = jnp.minimum(donor - 1, bound - receiver)
    shifted = jax.random.randint(jax.random.fold_in(rng, 1), (pairs,), 0, 1 << 20) % (room + 1)
    lengths = lengths.at[1:1 + 2 * pairs:2].set(donor - shifted).at[2:2 + 2 * pairs:2].set(receiver + shifted)
    return lengths[jax.random.permutation(jax.random.fold_in(rng, 2), count)]


def centred(rng, extent, spread, reach, cuts=(), kind=jnp.bfloat16):
    values = spread * jax.random.normal(rng, extent, jnp.float32)
    if cuts:
        values = values * level_of(rng, extent, cuts, -0.22, 0.18)
    return jnp.clip(values, -reach, reach).astype(kind)


def setup_inputs(seed: int = 0) -> dict:
    key_list = jax.random.split(jax.random.key(seed), 11)
    queries = draw_queries(jax.random.fold_in(key_list[10], 71), 0)
    keys = draw_keys(jax.random.fold_in(key_list[10], 71), 0)
    values = centred(key_list[2], (TOKENS, KVH * HD), 1.0, 6.0, ((0, 32),))
    resid = draw_resid(jax.random.fold_in(key_list[10], 71), 0)
    seg_ids = jnp.searchsorted(jnp.cumsum(uneven(key_list[4], DOCS, TOKENS, LEN // 2, 1)), jnp.arange(TOKENS), side="right").astype(jnp.int32)
    norm_gain = jnp.clip(1.0 + 0.18 * jax.random.normal(key_list[5], (D,), jnp.float32), 0.1, 1.9)
    expert_ids = draw_expert_ids(jax.random.fold_in(key_list[10], 71), 0)
    gate_weights = jnp.clip(0.1 + 0.79999997 * jax.random.uniform(key_list[7], (TOKENS,), jnp.float32) ** level_of(key_list[7], (TOKENS,), ((0, 32),), -0.2, 0.2), 0.1, 0.9)
    w_in = centred(key_list[8], (EXPERTS * SPLITS, D, 2 * FFS), D ** -0.5, 0.125, ((0, 32),))
    w_out = centred(key_list[9], (EXPERTS * SPLITS, FFS, D), FF ** -0.5, 0.21875, ((0, 32),))
    return {"queries": queries, "keys": keys, "values": values, "resid": resid, "seg_ids": seg_ids, "norm_gain": norm_gain, "expert_ids": expert_ids, "gate_weights": gate_weights, "w_in": w_in, "w_out": w_out}


def attend_row(packed):
    row_queries, row_keys, row_values, row_segments = packed
    scale_by = 1.0 / math.sqrt(HD)
    query_float = row_queries.astype(jnp.float32).reshape(LEN, KVH, HEAD_GROUP, HD)
    key_float = row_keys.astype(jnp.float32).reshape(LEN, KVH, HD)
    value_float = row_values.astype(jnp.float32).reshape(LEN, KVH, HD)
    scores = jnp.einsum('qhgd,khd->hgqk', query_float, key_float) * scale_by
    position = jnp.arange(LEN)
    allowed = (row_segments[:, None] == row_segments[None, :]) & (position[None, :] <= position[:, None])
    masked = jnp.where(allowed, scores, -jnp.inf)
    rowmax = lax.optimization_barrier(jnp.max(masked, axis=-1, keepdims=True))
    weights = jnp.where(allowed, jnp.exp(scores - rowmax), 0.0)
    totals = lax.optimization_barrier(jnp.sum(weights, axis=-1))
    rounded = lax.optimization_barrier(weights.astype(jnp.bfloat16)).astype(jnp.float32)
    mixture = jnp.einsum('hgqk,khd->qhgd', rounded, value_float) / jnp.transpose(totals, (2, 0, 1))[..., None]
    return mixture.reshape(LEN, HEADS * HD).astype(jnp.bfloat16)

def reference(queries, keys, values, resid, seg_ids, norm_gain, expert_ids, gate_weights, w_in, w_out):
    attended = lax.map(attend_row, (queries.reshape(N_EXP, LEN, HEADS * HD), keys.reshape(N_EXP, LEN, KVH * HD), values.reshape(N_EXP, LEN, KVH * HD), seg_ids.reshape(N_EXP, LEN)))
    attended = attended.reshape(TOKENS, HEADS * HD)
    hidden = (resid.astype(jnp.float32) + attended.astype(jnp.float32)).astype(jnp.bfloat16)
    hidden_float = hidden.astype(jnp.float32)
    meansq = lax.optimization_barrier(jnp.mean(hidden_float * hidden_float, axis=-1, keepdims=True))
    normed = (hidden_float * lax.rsqrt(meansq + 1e-06) * norm_gain).astype(jnp.bfloat16)
    capacity = SLOT_CAP * N_EXP * N_SEQ

    def expert_step(expert, running):
        expert = jnp.asarray(expert, jnp.int32)
        chosen = expert_ids == expert
        picked = jnp.nonzero(chosen, size=capacity, fill_value=0)[0].astype(jnp.int32)
        live_rows = jnp.arange(capacity) < jnp.sum(chosen.astype(jnp.int32))
        rows_in = normed[picked].astype(jnp.float32)
        first_row = (expert * SPLITS).astype(jnp.int32)
        stack_in = lax.dynamic_slice_in_dim(w_in, first_row, SPLITS, 0).astype(jnp.float32)
        stack_out = lax.dynamic_slice_in_dim(w_out, first_row, SPLITS, 0).astype(jnp.float32)
        gate_up = jnp.einsum('rd,qdf->qrf', rows_in, stack_in)
        active = jax.nn.silu(gate_up[..., :FFS]) * gate_up[..., FFS:]
        active = lax.optimization_barrier(active.astype(jnp.bfloat16)).astype(jnp.float32)
        partial_value = jnp.einsum('qrf,qfd->qrd', active, stack_out)
        partial_value = lax.optimization_barrier(partial_value.astype(jnp.bfloat16)).astype(jnp.float32)
        expert_out = lax.optimization_barrier(lax.optimization_barrier(jnp.sum(partial_value, axis=0)).astype(jnp.bfloat16)).astype(jnp.float32)
        expert_out = jnp.where(live_rows[:, None], expert_out, 0.0)
        return running.at[picked].add(expert_out)
    routed = lax.fori_loop(0, EXPERTS, expert_step, jnp.zeros((TOKENS, D), jnp.float32))
    return (hidden_float + gate_weights[:, None] * routed).astype(jnp.bfloat16)
```

```python
import functools
import math

import jax
import jax.numpy as jnp
from jax import lax
from jax.experimental import pallas as pl
from jax.experimental.pallas import tpu as pltpu
from jax.sharding import PartitionSpec as P

HD = 128
HEADS = 16
KVH = 2
EXP_DEV = 4
FF = 768
EPS = 1e-6
F32 = jnp.float32
BF16 = jnp.bfloat16
VMEM = pl.BlockSpec(memory_space=pltpu.VMEM)


def attend_kernel(
    blocks, splits, capacity, q_ref, *refs
):
    kv_refs = refs[:blocks]
    seg_q_ref, seg_k_ref, resid_ref, gain_ref, ids_col_ref, ids_row_ref = refs[blocks : blocks + 6]
    hidden_ref, outgoing_ref = refs[blocks + 6 :]
    rows = q_ref.shape[0]
    width = blocks * rows
    group = HEADS // KVH
    scale_by = 1.0 / math.sqrt(HD)
    key_at = lax.broadcasted_iota(jnp.int32, (rows, width), 1) - (width - rows)
    query_at = lax.broadcasted_iota(jnp.int32, (rows, width), 0)
    allowed = (seg_q_ref[...] == seg_k_ref[...]) & (key_at <= query_at)
    sumsq = jnp.zeros((rows, 1), F32)
    for kv_head in range(KVH):
        key_cols = slice(kv_head * HD, (kv_head + 1) * HD)
        value_cols = slice((KVH + kv_head) * HD, (KVH + kv_head + 1) * HD)
        head_keys = jnp.concatenate([ref[:, key_cols] for ref in kv_refs], 0)
        head_values = jnp.concatenate([ref[:, value_cols] for ref in kv_refs], 0)
        for head in range(kv_head * group, (kv_head + 1) * group):
            cols = slice(head * HD, (head + 1) * HD)
            scores = lax.dot_general(
                q_ref[:, cols], head_keys, (((1,), (1,)), ((), ())), preferred_element_type=F32
            )
            scores = jnp.where(allowed, scores * scale_by, -jnp.inf)
            weights = jnp.exp(scores - jnp.max(scores, axis=-1, keepdims=True))
            totals = jnp.sum(weights, axis=-1, keepdims=True)
            mixture = jnp.dot(weights.astype(BF16), head_values, preferred_element_type=F32)
            attended = (mixture / totals).astype(BF16).astype(F32)
            hidden = (resid_ref[:, cols].astype(F32) + attended).astype(BF16)
            hidden_ref[:, cols] = hidden
            hidden_float = hidden.astype(F32)
            sumsq += jnp.sum(hidden_float * hidden_float, axis=-1, keepdims=True)
    inverse = lax.rsqrt(sumsq / (HEADS * HD) + EPS)
    earlier = lax.broadcasted_iota(jnp.int32, (rows, rows), 0) < lax.broadcasted_iota(
        jnp.int32, (rows, rows), 1
    )
    same = (ids_col_ref[...] == ids_row_ref[...]) & earlier
    rank = jnp.sum(same.astype(F32), axis=0, keepdims=True).astype(jnp.int32)
    slots = outgoing_ref.shape[0]
    slot_at = lax.broadcasted_iota(jnp.int32, (slots, rows), 0)
    first = ids_row_ref[...] * (splits * capacity) + rank
    placing = slot_at == first
    for split in range(1, splits):
        placing = placing | (slot_at == first + split * capacity)
    placing = placing.astype(F32).astype(BF16)
    step = 512
    for low in range(0, HEADS * HD, step):
        cols = slice(low, low + step)
        normed = (hidden_ref[:, cols].astype(F32) * inverse * gain_ref[:, cols]).astype(BF16)
        outgoing_ref[:, cols] = jnp.dot(placing, normed, preferred_element_type=F32).astype(BF16)


def attend(splits, capacity, slots, queries, kv_blocks, seg_q, seg_k, resid, gain, ids):
    rows, model_width = resid.shape
    blocks = len(kv_blocks)
    return pl.pallas_call(
        functools.partial(attend_kernel, blocks, splits, capacity),
        out_shape=(
            jax.ShapeDtypeStruct((rows, model_width), BF16),
            jax.ShapeDtypeStruct((slots, model_width), BF16),
        ),
        in_specs=[VMEM] * (blocks + 7),
        out_specs=(VMEM, VMEM),
        compiler_params=pltpu.CompilerParams(vmem_limit_bytes=32 * 2**20),
        name="attend",
    )(queries, *kv_blocks, seg_q, seg_k, resid, gain, ids[:, None], ids[None, :])


def expert_kernel(x_ref, gate_ref, up_ref, down_ref, out_ref, total):
    step = pl.program_id(0)
    rows_in = x_ref[...]
    gate = jnp.dot(rows_in, gate_ref[0], preferred_element_type=F32)
    up = jnp.dot(rows_in, up_ref[0], preferred_element_type=F32)
    active = (gate / (1.0 + jnp.exp(-gate)) * up).astype(BF16)
    part = jnp.dot(active, down_ref[0], preferred_element_type=F32)

    @pl.when(step == 0)
    def _():
        total[...] = part

    @pl.when(step > 0)
    def _():
        total[...] += part

    @pl.when(step == pl.num_programs(0) - 1)
    def _():
        out_ref[...] = total[...].astype(BF16)


def experts(rows_in, w_in, w_out):
    rows, model_width = rows_in.shape
    units = w_out.shape[1]
    tile = 256
    if units % tile:
        gate_up = jnp.dot(rows_in, w_in[0], preferred_element_type=F32)
        active = (jax.nn.silu(gate_up[:, :units]) * gate_up[:, units:]).astype(BF16)
        return jnp.dot(active, w_out[0], preferred_element_type=F32).astype(BF16)
    steps = units // tile
    return pl.pallas_call(
        expert_kernel,
        grid=(steps,),
        out_shape=jax.ShapeDtypeStruct((rows, model_width), BF16),
        in_specs=[
            pl.BlockSpec((rows, model_width), lambda i: (0, 0)),
            pl.BlockSpec((1, model_width, tile), lambda i: (0, 0, i)),
            pl.BlockSpec((1, model_width, tile), lambda i: (0, 0, steps + i)),
            pl.BlockSpec((1, tile, model_width), lambda i: (0, i, 0)),
        ],
        out_specs=pl.BlockSpec((rows, model_width), lambda i: (0, 0)),
        scratch_shapes=[pltpu.VMEM((rows, model_width), F32)],
        compiler_params=pltpu.CompilerParams(vmem_limit_bytes=40 * 2**20),
        name="experts",
    )(rows_in, w_in, w_in, w_out)


def combine_kernel(splits, capacity, delivered_ref, hidden_ref, gate_ref, ids_col_ref, ids_row_ref, out_ref):
    rows = hidden_ref.shape[0]
    slots = delivered_ref.shape[0]
    earlier = lax.broadcasted_iota(jnp.int32, (rows, rows), 1) < lax.broadcasted_iota(
        jnp.int32, (rows, rows), 0
    )
    same = (ids_col_ref[...] == ids_row_ref[...]) & earlier
    rank = jnp.sum(same.astype(F32), axis=1, keepdims=True).astype(jnp.int32)
    first = ids_col_ref[...] * (splits * capacity) + rank
    slot_at = lax.broadcasted_iota(jnp.int32, (rows, slots), 1)
    picking = slot_at == first
    for split in range(1, splits):
        picking = picking | (slot_at == first + split * capacity)
    picking = picking.astype(F32).astype(BF16)
    step = 512
    for low in range(0, hidden_ref.shape[1], step):
        cols = slice(low, low + step)
        routed = jnp.dot(picking, delivered_ref[:, cols], preferred_element_type=F32)
        routed = routed.astype(BF16).astype(F32)
        out_ref[:, cols] = (hidden_ref[:, cols].astype(F32) + gate_ref[...] * routed).astype(BF16)


def combine(splits, capacity, delivered, hidden, gates, ids):
    return pl.pallas_call(
        functools.partial(combine_kernel, splits, capacity),
        out_shape=jax.ShapeDtypeStruct(hidden.shape, BF16),
        in_specs=[VMEM] * 5,
        out_specs=VMEM,
        compiler_params=pltpu.CompilerParams(vmem_limit_bytes=32 * 2**20),
        name="combine",
    )(delivered, hidden, gates[:, None], ids[:, None], ids[None, :])


def per_device(
    queries, keys, values, resid, seg_ids, norm_gain, expert_ids, gate_weights, w_in, w_out
):
    seq_count = lax.axis_size("seq")
    exp_count = lax.axis_size("exp")
    devices = seq_count * exp_count
    rows, model_width = resid.shape
    length = rows * seq_count
    splits = FF // w_out.shape[1]
    capacity = max(2, 2 * rows * splits // devices)
    slots = devices * capacity
    reach = length // 2
    before = min(seq_count - 1, -(-(reach - 1) // rows))
    place = lax.axis_index("seq")

    own = jnp.concatenate([keys, values], axis=1)
    kv_blocks = [
        lax.ppermute(own, "seq", [(i, i + hop) for i in range(seq_count - hop)])
        for hop in range(before, 0, -1)
    ] + [own]
    padded = jnp.concatenate([jnp.full((before * rows,), -1, jnp.int32), seg_ids])
    window = lax.dynamic_slice(padded, (place * rows,), ((before + 1) * rows,))
    seg_q, seg_k = window[before * rows :, None], window[None, :]
    hidden, outgoing = attend(
        splits, capacity, slots, queries, kv_blocks, seg_q, seg_k, resid, norm_gain[None, :], expert_ids
    )

    def exchange(block):
        return lax.all_to_all(
            block.reshape(devices, capacity, model_width),
            ("exp", "seq"),
            split_axis=0,
            concat_axis=0,
            tiled=True,
        ).reshape(slots, model_width)

    delivered = exchange(experts(exchange(outgoing), w_in, w_out))
    return combine(splits, capacity, delivered, hidden, gate_weights, expert_ids)


def solution(mesh):
    placed = (
        P(("exp", "seq"), None),
        P(("exp", "seq"), None),
        P(("exp", "seq"), None),
        P(("exp", "seq"), None),
        P("exp"),
        P(),
        P(("exp", "seq")),
        P(("exp", "seq")),
        P(("exp", "seq"), None, None),
        P(("exp", "seq"), None, None),
    )
    return jax.shard_map(
        per_device, mesh=mesh, in_specs=placed, out_specs=P(("exp", "seq"), None), check_vma=False
    )
```

```python
import functools
import math

import jax
import jax.numpy as jnp
from jax import lax
from jax.experimental import pallas as pl
from jax.experimental.pallas import tpu as pltpu
from jax.sharding import PartitionSpec as P

HD = 128
HEADS = 16
KVH = 2
EXP_DEV = 4
FF = 768
EPS = 1e-6
F32 = jnp.float32
BF16 = jnp.bfloat16
VMEM = pl.BlockSpec(memory_space=pltpu.VMEM)
HBM = pl.BlockSpec(memory_space=pltpu.HBM)
SCALE = 1.0 / math.sqrt(HD)
GROUP = HEADS // KVH
MIB = 2**20


def head_cols(head):
    return slice(head * HD, (head + 1) * HD)


def iota(shape, dimension):
    return lax.broadcasted_iota(jnp.int32, shape, dimension)


def as_column(row):
    count = row.shape[1]
    square = jnp.broadcast_to(row, (count, count))
    eye = iota((count, count), 0) == iota((count, count), 1)
    kept = jnp.where(eye, square, jnp.zeros_like(square))
    if row.dtype == jnp.int32:
        return jnp.sum(kept.astype(F32), axis=1, keepdims=True).astype(jnp.int32)
    return jnp.sum(kept, axis=1, keepdims=True)


def stage_kernel(before, splits, capacity, *refs):
    count = 7
    sources, refs = refs[:count], refs[count:]
    copied, refs = refs[: count - 3], refs[count - 3 :]
    bias_ref, placing_ref, picking_ref, gates_ref, refs = *refs[:4], refs[4:]
    small, sems = refs[:3], refs[3]
    copies = [
        pltpu.make_async_copy(source, target, sems.at[i])
        for i, (source, target) in enumerate(zip(sources, (*small, *copied)))
    ]
    for copy in copies:
        copy.start()
    seg_ref, ids_ref, gate_row_ref = small
    for copy in copies[:3]:
        copy.wait()
    rows = bias_ref.shape[1]
    place = lax.axis_index("seq")

    def segments(hop):
        at = pl.multiple_of(jnp.maximum(place - hop, 0) * rows, rows)
        return jnp.where(place >= hop, seg_ref[:, pl.ds(at, rows)], -1)

    seg_q = segments(0)
    for block, hop in enumerate(range(before, -1, -1)):
        allowed = as_column(segments(hop)) == seg_q
        if hop == 0:
            allowed = allowed & (iota((rows, rows), 0) <= iota((rows, rows), 1))
        bias_ref[block * rows : (block + 1) * rows, :] = jnp.where(allowed, 0.0, -jnp.inf)
    slots = placing_ref.shape[0]
    ids_row = ids_ref[...]
    first = slots_of(ids_row, splits, capacity, 1)
    placing_ref[...] = one_hot(first, iota((slots, rows), 0), splits, capacity)
    first = slots_of(ids_row, splits, capacity, 0)
    picking_ref[...] = one_hot(first, iota((rows, slots), 1), splits, capacity)
    gates_ref[...] = jnp.broadcast_to(as_column(gate_row_ref[...]), gates_ref.shape)
    for copy in copies[3:]:
        copy.wait()


def stage(before, splits, capacity, slots, seg, ids, gates, *large):
    rows = large[0].shape[0]
    sources = (seg, ids, gates, *large)
    return pl.pallas_call(
        functools.partial(stage_kernel, before, splits, capacity),
        out_shape=(
            *[pltpu.VMEM(array.shape, array.dtype) for array in large],
            pltpu.VMEM(((before + 1) * rows, rows), F32),
            pltpu.VMEM((slots, rows), BF16),
            pltpu.VMEM((rows, slots), BF16),
            pltpu.VMEM((rows, rows), F32),
        ),
        in_specs=[HBM] * len(sources),
        out_specs=(VMEM,) * (len(large) + 4),
        scratch_shapes=[
            *[pltpu.VMEM(array.shape, array.dtype) for array in (seg, ids, gates)],
            pltpu.SemaphoreType.DMA((len(sources),)),
        ],
        compiler_params=pltpu.CompilerParams(vmem_limit_bytes=16 * MIB),
        cost_estimate=pl.CostEstimate(flops=0, bytes_accessed=10 * MIB, transcendentals=0),
        name="stage",
    )(*[pltpu.with_memory_space_constraint(array, pltpu.HBM) for array in sources])


def slots_of(ids_row, splits, capacity, axis):
    count = ids_row.shape[1]
    ids_col = as_column(ids_row)
    earlier = iota((count, count), 1 - axis) < iota((count, count), axis)
    same = ((ids_col == ids_row) & earlier).astype(F32)
    rank = jnp.sum(same, axis=1 - axis, keepdims=True).astype(jnp.int32)
    return (ids_row if axis == 1 else ids_col) * (splits * capacity) + rank


def one_hot(first, slot_at, splits, capacity):
    hot = slot_at == first
    for split in range(1, splits):
        hot = hot | (slot_at == first + split * capacity)
    return hot.astype(F32).astype(BF16)


def attend_kernel(blocks, *refs):
    key_refs, value_refs, refs = refs[:blocks], refs[blocks : 2 * blocks], refs[2 * blocks :]
    q_ref, resid_ref, gain_ref, bias_ref, placing_ref, hidden_ref, outgoing_ref = refs[:7]
    score_ref, weight_ref, turn_ref = refs[7:]
    rows = q_ref.shape[0]
    eye = (iota((rows, rows), 0) == iota((rows, rows), 1)).astype(F32).astype(BF16)
    by_rows = (((1,), (1,)), ((), ()))
    pairs = HEADS // 2
    kv_of = [2 * pair // GROUP for pair in range(pairs)]
    bias = jnp.concatenate([bias_ref[...]] * 2, 1)
    head_keys = [
        jnp.concatenate([ref[:, head_cols(kv_head)] for ref in key_refs], 0)
        for kv_head in range(KVH)
    ]
    for pair in range(pairs):
        pair_queries = jnp.concatenate([q_ref[:, head_cols(2 * pair + i)] for i in range(2)], 0)
        products = lax.dot_general(
            head_keys[kv_of[pair]], pair_queries, by_rows, preferred_element_type=F32
        )
        score_ref[pair] = products * SCALE + bias
    values_t = [
        jnp.concatenate(
            [
                lax.dot_general(
                    eye,
                    ref[:, head_cols(ref.shape[1] // HD - KVH + kv_head)],
                    by_rows,
                    preferred_element_type=F32,
                ).astype(BF16)
                for ref in value_refs
            ],
            1,
        )
        for kv_head in range(KVH)
    ]
    totals = []
    for pair in range(pairs):
        scores = score_ref[pair]
        weights = jnp.exp(scores - jnp.max(scores, axis=0, keepdims=True))
        totals.append(jnp.sum(weights, axis=0, keepdims=True))
        weight_ref[pair] = weights.astype(BF16)
    for pair in range(pairs):
        mixture = jnp.dot(values_t[kv_of[pair]], weight_ref[pair], preferred_element_type=F32)
        attended = (mixture * (1.0 / totals[pair])).astype(BF16)
        for i in range(2):
            turn_ref[head_cols(2 * pair + i), :] = attended[:, i * rows : (i + 1) * rows]
    step = 512
    squares = jnp.zeros((rows, HD), F32)
    for low in range(0, HEADS * HD, step):
        cols = slice(low, low + step)
        attended = lax.dot_general(eye, turn_ref[cols, :], by_rows, preferred_element_type=F32)
        hidden = (resid_ref[:, cols].astype(F32) + attended).astype(BF16)
        hidden_ref[:, cols] = hidden
        hidden_float = hidden.astype(F32)
        square = hidden_float * hidden_float
        for at in range(0, step, HD):
            squares += square[:, at : at + HD]
    sumsq = jnp.sum(squares, axis=-1, keepdims=True)
    inverse = jnp.broadcast_to(lax.rsqrt(sumsq / (HEADS * HD) + EPS), (rows, step))
    placing = placing_ref[...]
    for low in range(0, HEADS * HD, step):
        cols = slice(low, low + step)
        normed = (hidden_ref[:, cols].astype(F32) * inverse * gain_ref[:, cols]).astype(BF16)
        outgoing_ref[:, cols] = jnp.dot(placing, normed, preferred_element_type=F32).astype(BF16)


def attend(keys, values, queries, resid, gain, bias, placing):
    rows, model_width = resid.shape
    slots = placing.shape[0]
    operands = (*keys, *values, queries, resid, gain, bias, placing)
    return pl.pallas_call(
        functools.partial(attend_kernel, len(keys)),
        out_shape=(
            pltpu.VMEM((rows, model_width), BF16),
            pltpu.VMEM((slots, model_width), BF16),
        ),
        in_specs=[VMEM] * len(operands),
        out_specs=(VMEM, VMEM),
        scratch_shapes=[
            pltpu.VMEM((HEADS // 2, len(keys) * rows, 2 * rows), F32),
            pltpu.VMEM((HEADS // 2, len(keys) * rows, 2 * rows), BF16),
            pltpu.VMEM((model_width, rows), BF16),
        ],
        compiler_params=pltpu.CompilerParams(vmem_limit_bytes=32 * MIB),
        name="attend",
    )(*operands)


def expert_kernel(x_ref, in_ref, down_ref, out_ref, active_ref):
    units = down_ref.shape[1]
    tile = 256
    rows_in = x_ref[...]
    for low in range(0, units, tile):
        gate = jnp.dot(rows_in, in_ref[0, :, low : low + tile], preferred_element_type=F32)
        up_cols = slice(units + low, units + low + tile)
        up = jnp.dot(rows_in, in_ref[0, :, up_cols], preferred_element_type=F32)
        active_ref[:, low : low + tile] = (gate / (1.0 + jnp.exp(-gate)) * up).astype(BF16)
    active = active_ref[...]
    step = 512
    for low in range(0, out_ref.shape[1], step):
        cols = slice(low, low + step)
        out_ref[:, cols] = jnp.dot(
            active, down_ref[0, :, cols], preferred_element_type=F32
        ).astype(BF16)


def experts(rows_in, w_in, w_out):
    rows, model_width = rows_in.shape
    units = w_out.shape[1]
    if units % 256:
        gate_up = jnp.dot(rows_in, w_in[0], preferred_element_type=F32)
        active = (jax.nn.silu(gate_up[:, :units]) * gate_up[:, units:]).astype(BF16)
        return jnp.dot(active, w_out[0], preferred_element_type=F32).astype(BF16)
    return pl.pallas_call(
        expert_kernel,
        out_shape=jax.ShapeDtypeStruct((rows, model_width), BF16),
        in_specs=[VMEM] * 3,
        out_specs=VMEM,
        scratch_shapes=[pltpu.VMEM((rows, units), BF16)],
        compiler_params=pltpu.CompilerParams(vmem_limit_bytes=16 * MIB),
        name="experts",
    )(rows_in, w_in, w_out)


def combine_kernel(delivered_ref, hidden_ref, picking_ref, gates_ref, out_ref):
    step = 512
    gates = jnp.concatenate([gates_ref[...]] * (step // gates_ref.shape[1]), 1)
    for low in range(0, hidden_ref.shape[1], step):
        cols = slice(low, low + step)
        routed = jnp.dot(picking_ref[...], delivered_ref[:, cols], preferred_element_type=F32)
        routed = routed.astype(BF16).astype(F32)
        out_ref[:, cols] = (hidden_ref[:, cols].astype(F32) + gates * routed).astype(BF16)


def combine(delivered, hidden, picking, gates):
    return pl.pallas_call(
        combine_kernel,
        out_shape=jax.ShapeDtypeStruct(hidden.shape, BF16),
        in_specs=[VMEM] * 4,
        out_specs=VMEM,
        compiler_params=pltpu.CompilerParams(vmem_limit_bytes=16 * MIB),
        name="combine",
    )(delivered, hidden, picking, gates)


def per_device(
    queries, keys, values, resid, seg_ids, norm_gain, expert_ids, gate_weights, w_in, w_out
):
    seq_count = lax.axis_size("seq")
    exp_count = lax.axis_size("exp")
    devices = seq_count * exp_count
    rows, model_width = resid.shape
    length = rows * seq_count
    splits = FF // w_out.shape[1]
    capacity = max(2, 2 * rows * splits // devices)
    slots = devices * capacity
    reach = length // 2
    before = min(seq_count - 1, -(-(reach - 1) // rows))

    own = jnp.concatenate([keys, values], axis=1)
    blocks = [
        lax.ppermute(own, "seq", [(i, i + hop) for i in range(seq_count - hop)])
        for hop in range(before, 0, -1)
    ]
    queries, resid, w_in, w_out, bias, placing, picking, gates = stage(
        before, splits, capacity, slots, seg_ids[None], expert_ids[None], gate_weights[None],
        queries, resid, w_in, w_out,
    )
    hidden, outgoing = attend([*blocks, keys], [*blocks, values], queries, resid, norm_gain[None], bias, placing)

    def exchange(block):
        return lax.all_to_all(
            block.reshape(devices, capacity, model_width),
            ("exp", "seq"),
            split_axis=0,
            concat_axis=0,
            tiled=True,
        ).reshape(slots, model_width)

    delivered = exchange(experts(exchange(outgoing), w_in, w_out))
    return combine(delivered, hidden, picking, gates)


def solution(mesh):
    placed = (
        P(("exp", "seq"), None),
        P(("exp", "seq"), None),
        P(("exp", "seq"), None),
        P(("exp", "seq"), None),
        P("exp"),
        P(),
        P(("exp", "seq")),
        P(("exp", "seq")),
        P(("exp", "seq"), None, None),
        P(("exp", "seq"), None, None),
    )
    return jax.shard_map(
        per_device, mesh=mesh, in_specs=placed, out_specs=P(("exp", "seq"), None), check_vma=False
    )
```

```python
import functools
import math

import jax
import jax.numpy as jnp
from jax import lax
from jax.experimental import pallas as pl
from jax.experimental.pallas import tpu as pltpu
from jax.sharding import PartitionSpec as P

HD = 128
HEADS = 16
KVH = 2
EXP_DEV = 4
FF = 768
EPS = 1e-6
F32 = jnp.float32
BF16 = jnp.bfloat16
VMEM = pl.BlockSpec(memory_space=pltpu.VMEM)
HBM = pl.BlockSpec(memory_space=pltpu.HBM)
SCALE = 1.0 / math.sqrt(HD)
GROUP = HEADS // KVH
MIB = 2**20
PAIRS = HEADS // 2
BY_ROWS = (((1,), (1,)), ((), ()))


def head_cols(head):
    return slice(head * HD, (head + 1) * HD)


def iota(shape, dimension):
    return lax.broadcasted_iota(jnp.int32, shape, dimension)


def as_column(row):
    count = row.shape[1]
    square = jnp.broadcast_to(row, (count, count))
    eye = iota((count, count), 0) == iota((count, count), 1)
    kept = jnp.where(eye, square, jnp.zeros_like(square))
    if row.dtype == jnp.int32:
        return jnp.sum(kept.astype(F32), axis=1, keepdims=True).astype(jnp.int32)
    return jnp.sum(kept, axis=1, keepdims=True)


def stage_kernel(before, splits, capacity, *refs):
    count = 7
    sources, refs = refs[:count], refs[count:]
    copied, refs = refs[: count - 3], refs[count - 3 :]
    bias_ref, placing_ref, picking_ref, gates_ref, refs = *refs[:4], refs[4:]
    small, sems = refs[:3], refs[3]
    copies = [
        pltpu.make_async_copy(source, target, sems.at[i])
        for i, (source, target) in enumerate(zip(sources, (*small, *copied)))
    ]
    for copy in copies:
        copy.start()
    seg_ref, ids_ref, gate_row_ref = small
    for copy in copies[:3]:
        copy.wait()
    rows = bias_ref.shape[1]
    place = lax.axis_index("seq")

    def segments(hop):
        at = pl.multiple_of(jnp.maximum(place - hop, 0) * rows, rows)
        return jnp.where(place >= hop, seg_ref[:, pl.ds(at, rows)], -1)

    seg_q = segments(0)
    for block, hop in enumerate(range(before, -1, -1)):
        allowed = as_column(segments(hop)) == seg_q
        if hop == 0:
            allowed = allowed & (iota((rows, rows), 0) <= iota((rows, rows), 1))
        bias_ref[block * rows : (block + 1) * rows, :] = jnp.where(allowed, 0.0, -jnp.inf)
    slots = placing_ref.shape[0]
    ids_row = ids_ref[...]
    first = slots_of(ids_row, splits, capacity, 1)
    placing_ref[...] = one_hot(first, iota((slots, rows), 0), splits, capacity)
    first = slots_of(ids_row, splits, capacity, 0)
    picking_ref[...] = one_hot(first, iota((rows, slots), 1), splits, capacity)
    gates_ref[...] = jnp.broadcast_to(as_column(gate_row_ref[...]), gates_ref.shape)
    for copy in copies[3:]:
        copy.wait()


def stage(before, splits, capacity, slots, seg, ids, gates, *large):
    rows = large[0].shape[0]
    sources = (seg, ids, gates, *large)
    return pl.pallas_call(
        functools.partial(stage_kernel, before, splits, capacity),
        out_shape=(
            *[pltpu.VMEM(array.shape, array.dtype) for array in large],
            pltpu.VMEM(((before + 1) * rows, rows), F32),
            pltpu.VMEM((slots, rows), BF16),
            pltpu.VMEM((rows, slots), BF16),
            pltpu.VMEM((rows, rows), F32),
        ),
        in_specs=[HBM] * len(sources),
        out_specs=(VMEM,) * (len(large) + 4),
        scratch_shapes=[
            *[pltpu.VMEM(array.shape, array.dtype) for array in (seg, ids, gates)],
            pltpu.SemaphoreType.DMA((len(sources),)),
        ],
        compiler_params=pltpu.CompilerParams(vmem_limit_bytes=16 * MIB),
        cost_estimate=pl.CostEstimate(flops=0, bytes_accessed=10 * MIB, transcendentals=0),
        name="stage",
    )(*[pltpu.with_memory_space_constraint(array, pltpu.HBM) for array in sources])


def slots_of(ids_row, splits, capacity, axis):
    count = ids_row.shape[1]
    ids_col = as_column(ids_row)
    earlier = iota((count, count), 1 - axis) < iota((count, count), axis)
    same = ((ids_col == ids_row) & earlier).astype(F32)
    rank = jnp.sum(same, axis=1 - axis, keepdims=True).astype(jnp.int32)
    return (ids_row if axis == 1 else ids_col) * (splits * capacity) + rank


def one_hot(first, slot_at, splits, capacity):
    hot = slot_at == first
    for split in range(1, splits):
        hot = hot | (slot_at == first + split * capacity)
    return hot.astype(F32).astype(BF16)


def weigh_kernel(blocks, *refs):
    key_refs, (q_ref, bias_ref, weight_ref, totals_ref, score_ref) = refs[:blocks], refs[blocks:]
    bias = jnp.concatenate([bias_ref[...]] * 2, 1)
    head_keys = [
        jnp.concatenate([ref[:, head_cols(kv_head)] for ref in key_refs], 0)
        for kv_head in range(KVH)
    ]
    for pair in range(PAIRS):
        pair_queries = jnp.concatenate([q_ref[:, head_cols(2 * pair + i)] for i in range(2)], 0)
        products = lax.dot_general(
            head_keys[2 * pair // GROUP], pair_queries, BY_ROWS, preferred_element_type=F32
        )
        score_ref[pair] = products * SCALE + bias
    for pair in range(PAIRS):
        scores = score_ref[pair]
        weights = jnp.exp(scores - jnp.max(scores, axis=0, keepdims=True))
        totals_ref[pair : pair + 1, :] = jnp.sum(weights, axis=0, keepdims=True)
        weight_ref[pair] = weights.astype(BF16)


def weigh(keys, queries, bias):
    rows = queries.shape[0]
    shape = (PAIRS, len(keys) * rows, 2 * rows)
    operands = (*keys, queries, bias)
    return pl.pallas_call(
        functools.partial(weigh_kernel, len(keys)),
        out_shape=(pltpu.VMEM(shape, BF16), pltpu.VMEM((PAIRS, 2 * rows), F32)),
        in_specs=[VMEM] * len(operands),
        out_specs=(VMEM, VMEM),
        scratch_shapes=[pltpu.VMEM(shape, F32)],
        compiler_params=pltpu.CompilerParams(vmem_limit_bytes=24 * MIB),
        cost_estimate=pl.CostEstimate(
            flops=4 * len(keys) * rows * rows * HEADS * HD, bytes_accessed=MIB, transcendentals=0
        ),
        name="weigh",
    )(*operands)


def mix_kernel(blocks, *refs):
    value_refs, refs = refs[:blocks], refs[blocks:]
    weight_ref, totals_ref, resid_ref, gain_ref, placing_ref = refs[:5]
    hidden_ref, outgoing_ref, turn_ref = refs[5:]
    rows = resid_ref.shape[0]
    eye = (iota((rows, rows), 0) == iota((rows, rows), 1)).astype(F32).astype(BF16)

    def turned(block):
        return lax.dot_general(eye, block, BY_ROWS, preferred_element_type=F32)

    values_t = [
        jnp.concatenate(
            [turned(ref[:, head_cols(kv_head)]).astype(BF16) for ref in value_refs], 1
        )
        for kv_head in range(KVH)
    ]
    scale = 1.0 / totals_ref[...]
    for pair in range(PAIRS):
        mixture = jnp.dot(
            values_t[2 * pair // GROUP], weight_ref[pair], preferred_element_type=F32
        )
        attended = (mixture * scale[pair : pair + 1, :]).astype(BF16)
        for i in range(2):
            turn_ref[head_cols(2 * pair + i), :] = attended[:, i * rows : (i + 1) * rows]
    step = 512
    squares = jnp.zeros((rows, HD), F32)
    for low in range(0, HEADS * HD, step):
        cols = slice(low, low + step)
        attended = turned(turn_ref[cols, :])
        hidden = (resid_ref[:, cols].astype(F32) + attended).astype(BF16)
        hidden_ref[:, cols] = hidden
        hidden_float = hidden.astype(F32)
        square = hidden_float * hidden_float
        for at in range(0, step, HD):
            squares += square[:, at : at + HD]
    sumsq = jnp.sum(squares, axis=-1, keepdims=True)
    inverse = jnp.broadcast_to(lax.rsqrt(sumsq / (HEADS * HD) + EPS), (rows, step))
    placing = placing_ref[...]
    for low in range(0, HEADS * HD, step):
        cols = slice(low, low + step)
        normed = (hidden_ref[:, cols].astype(F32) * inverse * gain_ref[:, cols]).astype(BF16)
        outgoing_ref[:, cols] = jnp.dot(placing, normed, preferred_element_type=F32).astype(BF16)


def mix(values, weights, totals, resid, gain, placing):
    rows, model_width = resid.shape
    operands = (*values, weights, totals, resid, gain, placing)
    return pl.pallas_call(
        functools.partial(mix_kernel, len(values)),
        out_shape=(
            pltpu.VMEM((rows, model_width), BF16),
            pltpu.VMEM((placing.shape[0], model_width), BF16),
        ),
        in_specs=[VMEM] * len(operands),
        out_specs=(VMEM, VMEM),
        scratch_shapes=[pltpu.VMEM((model_width, rows), BF16)],
        compiler_params=pltpu.CompilerParams(vmem_limit_bytes=16 * MIB),
        name="mix",
    )(*operands)


def expert_kernel(x_ref, in_ref, down_ref, out_ref, active_ref):
    units = down_ref.shape[1]
    tile = 256
    rows_in = x_ref[...]
    for low in range(0, units, tile):
        gate = jnp.dot(rows_in, in_ref[0, :, low : low + tile], preferred_element_type=F32)
        up_cols = slice(units + low, units + low + tile)
        up = jnp.dot(rows_in, in_ref[0, :, up_cols], preferred_element_type=F32)
        active_ref[:, low : low + tile] = (gate / (1.0 + jnp.exp(-gate)) * up).astype(BF16)
    active = active_ref[...]
    step = 512
    for low in range(0, out_ref.shape[1], step):
        cols = slice(low, low + step)
        out_ref[:, cols] = jnp.dot(
            active, down_ref[0, :, cols], preferred_element_type=F32
        ).astype(BF16)


def experts(rows_in, w_in, w_out):
    rows, model_width = rows_in.shape
    units = w_out.shape[1]
    if units % 256:
        gate_up = jnp.dot(rows_in, w_in[0], preferred_element_type=F32)
        active = (jax.nn.silu(gate_up[:, :units]) * gate_up[:, units:]).astype(BF16)
        return jnp.dot(active, w_out[0], preferred_element_type=F32).astype(BF16)
    return pl.pallas_call(
        expert_kernel,
        out_shape=jax.ShapeDtypeStruct((rows, model_width), BF16),
        in_specs=[VMEM] * 3,
        out_specs=VMEM,
        scratch_shapes=[pltpu.VMEM((rows, units), BF16)],
        compiler_params=pltpu.CompilerParams(vmem_limit_bytes=16 * MIB),
        name="experts",
    )(rows_in, w_in, w_out)


def combine_kernel(delivered_ref, hidden_ref, picking_ref, gates_ref, out_ref):
    step = 512
    gates = jnp.concatenate([gates_ref[...]] * (step // gates_ref.shape[1]), 1)
    for low in range(0, hidden_ref.shape[1], step):
        cols = slice(low, low + step)
        routed = jnp.dot(picking_ref[...], delivered_ref[:, cols], preferred_element_type=F32)
        routed = routed.astype(BF16).astype(F32)
        out_ref[:, cols] = (hidden_ref[:, cols].astype(F32) + gates * routed).astype(BF16)


def combine(delivered, hidden, picking, gates):
    return pl.pallas_call(
        combine_kernel,
        out_shape=jax.ShapeDtypeStruct(hidden.shape, BF16),
        in_specs=[VMEM] * 4,
        out_specs=VMEM,
        compiler_params=pltpu.CompilerParams(vmem_limit_bytes=16 * MIB),
        name="combine",
    )(delivered, hidden, picking, gates)


def per_device(
    queries, keys, values, resid, seg_ids, norm_gain, expert_ids, gate_weights, w_in, w_out
):
    seq_count = lax.axis_size("seq")
    exp_count = lax.axis_size("exp")
    devices = seq_count * exp_count
    rows, model_width = resid.shape
    length = rows * seq_count
    splits = FF // w_out.shape[1]
    capacity = max(2, 2 * rows * splits // devices)
    slots = devices * capacity
    reach = length // 2
    before = min(seq_count - 1, -(-(reach - 1) // rows))


    def earlier(own):
        return [
            lax.ppermute(own, "seq", [(i, (i + hop) % seq_count) for i in range(seq_count)])
            for hop in range(before, 0, -1)
        ]

    key_blocks, value_blocks = earlier(keys), earlier(values)
    queries, resid, w_in, w_out, bias, placing, picking, gates = stage(
        before, splits, capacity, slots, seg_ids[None], expert_ids[None], gate_weights[None],
        queries, resid, w_in, w_out,
    )
    weights, totals = weigh([*key_blocks, keys], queries, bias)
    hidden, outgoing = mix([*value_blocks, values], weights, totals, resid, norm_gain[None], placing)

    def exchange(block):
        return lax.all_to_all(
            block.reshape(devices, capacity, model_width),
            ("exp", "seq"),
            split_axis=0,
            concat_axis=0,
            tiled=True,
        ).reshape(slots, model_width)

    delivered = exchange(experts(exchange(outgoing), w_in, w_out))
    return combine(delivered, hidden, picking, gates)


def solution(mesh):
    placed = (
        P(("exp", "seq"), None),
        P(("exp", "seq"), None),
        P(("exp", "seq"), None),
        P(("exp", "seq"), None),
        P("exp"),
        P(),
        P(("exp", "seq")),
        P(("exp", "seq")),
        P(("exp", "seq"), None, None),
        P(("exp", "seq"), None, None),
    )
    return jax.shard_map(
        per_device, mesh=mesh, in_specs=placed, out_specs=P(("exp", "seq"), None), check_vma=False
    )
```

```python
import functools
import math

import jax
import jax.numpy as jnp
from jax import lax
from jax.experimental import pallas as pl
from jax.experimental.pallas import tpu as pltpu
from jax.sharding import PartitionSpec as P

HD = 128
HEADS = 16
KVH = 2
EXP_DEV = 4
FF = 768
EPS = 1e-6
F32 = jnp.float32
BF16 = jnp.bfloat16
VMEM = pl.BlockSpec(memory_space=pltpu.VMEM)
HBM = pl.BlockSpec(memory_space=pltpu.HBM)
SCALE = 1.0 / math.sqrt(HD)
GROUP = HEADS // KVH
MIB = 2**20
STAGED = 9
PAIRS = HEADS // 2
BY_ROWS = (((1,), (1,)), ((), ()))


def head_cols(head):
    return slice(head * HD, (head + 1) * HD)


def iota(shape, dimension):
    return lax.broadcasted_iota(jnp.int32, shape, dimension)


def as_column(row):
    count = row.shape[1]
    square = jnp.broadcast_to(row, (count, count))
    eye = iota((count, count), 0) == iota((count, count), 1)
    kept = jnp.where(eye, square, jnp.zeros_like(square))
    if row.dtype == jnp.int32:
        return jnp.sum(kept.astype(F32), axis=1, keepdims=True).astype(jnp.int32)
    return jnp.sum(kept, axis=1, keepdims=True)


def pieces(source, target):
    axis, count = source.ndim - 2, source.shape[-2]
    parts = max(1, source.size // MIB)
    while count % (16 * parts):
        parts -= 1
    step = count // parts
    for low in range(0, count, step):
        at = (0,) * axis + (slice(low, low + step),)
        yield source.at[at], target.at[at]


def stage_kernel(before, splits, capacity, *refs):
    count = STAGED
    sources, refs = refs[:count], refs[count:]
    copied, refs = refs[: count - 3], refs[count - 3 :]
    bias_ref, placing_ref, picking_ref, gates_ref, refs = *refs[:4], refs[4:]
    small, sems = refs[:3], refs[3]
    copies = []
    for source, target in zip(sources, (*small, *copied)):
        whole = source.shape[-2] % 16 != 0
        for part, place_for in [(source, target)] if whole else pieces(source, target):
            copies.append(pltpu.make_async_copy(part, place_for, sems.at[len(copies)]))
    for copy in copies:
        copy.start()
    seg_ref, ids_ref, gate_row_ref = small
    for copy in copies[:3]:
        copy.wait()
    rows = bias_ref.shape[1]
    place = lax.axis_index("seq")

    def segments(hop):
        at = pl.multiple_of(jnp.maximum(place - hop, 0) * rows, rows)
        return jnp.where(place >= hop, seg_ref[:, pl.ds(at, rows)], -1)

    seg_q = segments(0)
    for block, hop in enumerate(range(before, -1, -1)):
        allowed = as_column(segments(hop)) == seg_q
        if hop == 0:
            allowed = allowed & (iota((rows, rows), 0) <= iota((rows, rows), 1))
        bias_ref[block * rows : (block + 1) * rows, :] = jnp.where(allowed, 0.0, -jnp.inf)
    slots = placing_ref.shape[0]
    ids_row = ids_ref[...]
    first = slots_of(ids_row, splits, capacity, 1)
    placing_ref[...] = one_hot(first, iota((slots, rows), 0), splits, capacity)
    first = slots_of(ids_row, splits, capacity, 0)
    picking_ref[...] = one_hot(first, iota((rows, slots), 1), splits, capacity)
    gates_ref[...] = jnp.broadcast_to(as_column(gate_row_ref[...]), gates_ref.shape)
    for copy in copies[3:]:
        copy.wait()


def stage(before, splits, capacity, slots, seg, ids, gates, *large):
    rows = large[0].shape[0]
    sources = (seg, ids, gates, *large)
    return pl.pallas_call(
        functools.partial(stage_kernel, before, splits, capacity),
        out_shape=(
            *[pltpu.VMEM(array.shape, array.dtype) for array in large],
            pltpu.VMEM(((before + 1) * rows, rows), F32),
            pltpu.VMEM((slots, rows), BF16),
            pltpu.VMEM((rows, slots), BF16),
            pltpu.VMEM((rows, rows), F32),
        ),
        in_specs=[HBM] * len(sources),
        out_specs=(VMEM,) * (len(large) + 4),
        scratch_shapes=[
            *[pltpu.VMEM(array.shape, array.dtype) for array in (seg, ids, gates)],
            pltpu.SemaphoreType.DMA((32,)),
        ],
        compiler_params=pltpu.CompilerParams(vmem_limit_bytes=16 * MIB),
        cost_estimate=pl.CostEstimate(flops=0, bytes_accessed=10 * MIB, transcendentals=0),
        name="stage",
    )(*[pltpu.with_memory_space_constraint(array, pltpu.HBM) for array in sources])


def slots_of(ids_row, splits, capacity, axis):
    count = ids_row.shape[1]
    ids_col = as_column(ids_row)
    earlier = iota((count, count), 1 - axis) < iota((count, count), axis)
    same = ((ids_col == ids_row) & earlier).astype(F32)
    rank = jnp.sum(same, axis=1 - axis, keepdims=True).astype(jnp.int32)
    return (ids_row if axis == 1 else ids_col) * (splits * capacity) + rank


def one_hot(first, slot_at, splits, capacity):
    hot = slot_at == first
    for split in range(1, splits):
        hot = hot | (slot_at == first + split * capacity)
    return hot.astype(F32).astype(BF16)


def weigh_kernel(blocks, *refs):
    key_refs, (q_ref, bias_ref, weight_ref, totals_ref, score_ref) = refs[:blocks], refs[blocks:]
    bias = jnp.concatenate([bias_ref[...]] * 2, 1)
    head_keys = [
        jnp.concatenate([ref[:, head_cols(kv_head)] for ref in key_refs], 0)
        for kv_head in range(KVH)
    ]
    for pair in range(PAIRS):
        pair_queries = jnp.concatenate([q_ref[:, head_cols(2 * pair + i)] for i in range(2)], 0)
        products = lax.dot_general(
            head_keys[2 * pair // GROUP], pair_queries, BY_ROWS, preferred_element_type=F32
        )
        score_ref[pair] = products * SCALE + bias
    for pair in range(PAIRS):
        scores = score_ref[pair]
        weights = jnp.exp(scores - jnp.max(scores, axis=0, keepdims=True))
        totals_ref[pair : pair + 1, :] = jnp.sum(weights, axis=0, keepdims=True)
        weight_ref[pair] = weights.astype(BF16)


def weigh(keys, queries, bias):
    rows = queries.shape[0]
    shape = (PAIRS, len(keys) * rows, 2 * rows)
    operands = (*keys, queries, bias)
    return pl.pallas_call(
        functools.partial(weigh_kernel, len(keys)),
        out_shape=(pltpu.VMEM(shape, BF16), pltpu.VMEM((PAIRS, 2 * rows), F32)),
        in_specs=[VMEM] * len(operands),
        out_specs=(VMEM, VMEM),
        scratch_shapes=[pltpu.VMEM(shape, F32)],
        compiler_params=pltpu.CompilerParams(vmem_limit_bytes=24 * MIB),
        cost_estimate=pl.CostEstimate(
            flops=4 * len(keys) * rows * rows * HEADS * HD, bytes_accessed=MIB, transcendentals=0
        ),
        name="weigh",
    )(*operands)


def mix_kernel(blocks, *refs):
    value_refs, refs = refs[:blocks], refs[blocks:]
    weight_ref, totals_ref, resid_ref, gain_ref, placing_ref = refs[:5]
    hidden_ref, outgoing_ref, turn_ref = refs[5:]
    rows = resid_ref.shape[0]
    eye = (iota((rows, rows), 0) == iota((rows, rows), 1)).astype(F32).astype(BF16)

    def turned(block):
        return lax.dot_general(eye, block, BY_ROWS, preferred_element_type=F32)

    values_t = [
        jnp.concatenate(
            [turned(ref[:, head_cols(kv_head)]).astype(BF16) for ref in value_refs], 1
        )
        for kv_head in range(KVH)
    ]
    scale = 1.0 / totals_ref[...]
    for pair in range(PAIRS):
        mixture = jnp.dot(
            values_t[2 * pair // GROUP], weight_ref[pair], preferred_element_type=F32
        )
        attended = (mixture * scale[pair : pair + 1, :]).astype(BF16)
        for i in range(2):
            turn_ref[head_cols(2 * pair + i), :] = attended[:, i * rows : (i + 1) * rows]
    step = 512
    squares = jnp.zeros((rows, HD), F32)
    for low in range(0, HEADS * HD, step):
        cols = slice(low, low + step)
        attended = turned(turn_ref[cols, :])
        hidden = (resid_ref[:, cols].astype(F32) + attended).astype(BF16)
        hidden_ref[:, cols] = hidden
        hidden_float = hidden.astype(F32)
        square = hidden_float * hidden_float
        for at in range(0, step, HD):
            squares += square[:, at : at + HD]
    sumsq = jnp.sum(squares, axis=-1, keepdims=True)
    inverse = jnp.broadcast_to(lax.rsqrt(sumsq / (HEADS * HD) + EPS), (rows, step))
    placing = placing_ref[...]
    for low in range(0, HEADS * HD, step):
        cols = slice(low, low + step)
        normed = (hidden_ref[:, cols].astype(F32) * inverse * gain_ref[:, cols]).astype(BF16)
        outgoing_ref[:, cols] = jnp.dot(placing, normed, preferred_element_type=F32).astype(BF16)


def mix(values, weights, totals, resid, gain, placing):
    rows, model_width = resid.shape
    operands = (*values, weights, totals, resid, gain, placing)
    return pl.pallas_call(
        functools.partial(mix_kernel, len(values)),
        out_shape=(
            pltpu.VMEM((rows, model_width), BF16),
            pltpu.VMEM((placing.shape[0], model_width), BF16),
        ),
        in_specs=[VMEM] * len(operands),
        out_specs=(VMEM, VMEM),
        scratch_shapes=[pltpu.VMEM((model_width, rows), BF16)],
        compiler_params=pltpu.CompilerParams(vmem_limit_bytes=16 * MIB),
        name="mix",
    )(*operands)


def expert_kernel(x_ref, in_ref, down_ref, out_ref, active_ref):
    units = down_ref.shape[1]
    tile = 256
    rows_in = x_ref[...]
    for low in range(0, units, tile):
        gate = jnp.dot(rows_in, in_ref[0, :, low : low + tile], preferred_element_type=F32)
        up_cols = slice(units + low, units + low + tile)
        up = jnp.dot(rows_in, in_ref[0, :, up_cols], preferred_element_type=F32)
        active_ref[:, low : low + tile] = (gate / (1.0 + jnp.exp(-gate)) * up).astype(BF16)
    active = active_ref[...]
    step = 512
    for low in range(0, out_ref.shape[1], step):
        cols = slice(low, low + step)
        out_ref[:, cols] = jnp.dot(
            active, down_ref[0, :, cols], preferred_element_type=F32
        ).astype(BF16)


def experts(rows_in, w_in, w_out):
    rows, model_width = rows_in.shape
    units = w_out.shape[1]
    if units % 256:
        gate_up = jnp.dot(rows_in, w_in[0], preferred_element_type=F32)
        active = (jax.nn.silu(gate_up[:, :units]) * gate_up[:, units:]).astype(BF16)
        return jnp.dot(active, w_out[0], preferred_element_type=F32).astype(BF16)
    return pl.pallas_call(
        expert_kernel,
        out_shape=jax.ShapeDtypeStruct((rows, model_width), BF16),
        in_specs=[VMEM] * 3,
        out_specs=VMEM,
        scratch_shapes=[pltpu.VMEM((rows, units), BF16)],
        compiler_params=pltpu.CompilerParams(vmem_limit_bytes=16 * MIB),
        name="experts",
    )(rows_in, w_in, w_out)


def combine_kernel(delivered_ref, hidden_ref, picking_ref, gates_ref, out_ref, made_ref, sems):
    step = 512
    gates = jnp.concatenate([gates_ref[...]] * (step // gates_ref.shape[1]), 1)
    picking = picking_ref[...]
    copies = []
    for low in range(0, hidden_ref.shape[1], step):
        cols = slice(low, low + step)
        routed = jnp.dot(picking, delivered_ref[:, cols], preferred_element_type=F32)
        routed = routed.astype(BF16).astype(F32)
        made_ref[:, cols] = (hidden_ref[:, cols].astype(F32) + gates * routed).astype(BF16)
        copies.append(
            pltpu.make_async_copy(made_ref.at[:, cols], out_ref.at[:, cols], sems.at[low // step])
        )
        copies[-1].start()
    for copy in copies:
        copy.wait()


def combine(delivered, hidden, picking, gates):
    return pl.pallas_call(
        combine_kernel,
        out_shape=pltpu.HBM(hidden.shape, BF16),
        in_specs=[VMEM] * 4,
        out_specs=HBM,
        scratch_shapes=[
            pltpu.VMEM(hidden.shape, BF16),
            pltpu.SemaphoreType.DMA((hidden.shape[1] // 512,)),
        ],
        compiler_params=pltpu.CompilerParams(vmem_limit_bytes=16 * MIB),
        name="combine",
    )(delivered, hidden, picking, gates)


def per_device(
    queries, keys, values, resid, seg_ids, norm_gain, expert_ids, gate_weights, w_in, w_out
):
    seq_count = lax.axis_size("seq")
    exp_count = lax.axis_size("exp")
    devices = seq_count * exp_count
    rows, model_width = resid.shape
    length = rows * seq_count
    splits = FF // w_out.shape[1]
    capacity = max(2, 2 * rows * splits // devices)
    slots = devices * capacity
    reach = length // 2
    before = min(seq_count - 1, -(-(reach - 1) // rows))


    def earlier(own):
        return [
            lax.ppermute(own, "seq", [(i, (i + hop) % seq_count if i + hop < seq_count else (seq_count - 1 - i) if hop == 2 else (i + hop) % seq_count) for i in range(seq_count)])
            for hop in range(before, 0, -1)
        ]

    key_blocks, value_blocks = earlier(keys), earlier(values)
    queries, keys, values, resid, gain, w_in, bias, placing, picking, gates = stage(
        before, splits, capacity, slots, seg_ids[None], expert_ids[None], gate_weights[None],
        queries, keys, values, resid, norm_gain[None], w_in,
    )
    weights, totals = weigh([*key_blocks, keys], queries, bias)
    hidden, outgoing = mix([*value_blocks, values], weights, totals, resid, gain, placing)

    def exchange(block):
        return lax.all_to_all(
            block.reshape(devices, capacity, model_width),
            ("exp", "seq"),
            split_axis=0,
            concat_axis=0,
            tiled=True,
        ).reshape(slots, model_width)

    delivered = exchange(experts(exchange(outgoing), w_in, w_out))
    return combine(delivered, hidden, picking, gates)


def solution(mesh):
    placed = (
        P(("exp", "seq"), None),
        P(("exp", "seq"), None),
        P(("exp", "seq"), None),
        P(("exp", "seq"), None),
        P("exp"),
        P(),
        P(("exp", "seq")),
        P(("exp", "seq")),
        P(("exp", "seq"), None, None),
        P(("exp", "seq"), None, None),
    )
    return jax.shard_map(
        per_device, mesh=mesh, in_specs=placed, out_specs=P(("exp", "seq"), None), check_vma=False
    )
```

```python
import functools
import math

import jax
import jax.numpy as jnp
from jax import lax
from jax.experimental import pallas as pl
from jax.experimental.pallas import tpu as pltpu
from jax.sharding import PartitionSpec as P

HD = 128
HEADS = 16
KVH = 2
EXP_DEV = 4
FF = 768
EPS = 1e-6
F32 = jnp.float32
BF16 = jnp.bfloat16
VMEM = pl.BlockSpec(memory_space=pltpu.VMEM)
HBM = pl.BlockSpec(memory_space=pltpu.HBM)
SCALE = 1.0 / math.sqrt(HD)
GROUP = HEADS // KVH
MIB = 2**20
STAGED = 9
PAIRS = HEADS // 2
BY_ROWS = (((1,), (1,)), ((), ()))


def head_cols(head):
    return slice(head * HD, (head + 1) * HD)


def iota(shape, dimension):
    return lax.broadcasted_iota(jnp.int32, shape, dimension)


def as_column(row):
    count = row.shape[1]
    square = jnp.broadcast_to(row, (count, count))
    eye = iota((count, count), 0) == iota((count, count), 1)
    kept = jnp.where(eye, square, jnp.zeros_like(square))
    if row.dtype == jnp.int32:
        return jnp.sum(kept.astype(F32), axis=1, keepdims=True).astype(jnp.int32)
    return jnp.sum(kept, axis=1, keepdims=True)


def pieces(source, target):
    axis, count = source.ndim - 2, source.shape[-2]
    parts = max(1, source.size // MIB)
    while count % (16 * parts):
        parts -= 1
    step = count // parts
    for low in range(0, count, step):
        at = (0,) * axis + (slice(low, low + step),)
        yield source.at[at], target.at[at]


def stage_kernel(before, splits, capacity, *refs):
    count = STAGED
    sources, refs = refs[:count], refs[count:]
    copied, refs = refs[: count - 3], refs[count - 3 :]
    bias_ref, placing_ref, picking_ref, gates_ref, refs = *refs[:4], refs[4:]
    small, sems = refs[:3], refs[3]
    copies = []
    for source, target in zip(sources, (*small, *copied)):
        whole = source.shape[-2] % 16 != 0
        for part, place_for in [(source, target)] if whole else pieces(source, target):
            copies.append(pltpu.make_async_copy(part, place_for, sems.at[len(copies)]))
    for copy in copies:
        copy.start()
    seg_ref, ids_ref, gate_row_ref = small
    for copy in copies[:3]:
        copy.wait()
    rows = bias_ref.shape[1]
    place = lax.axis_index("seq")

    def segments(hop):
        at = pl.multiple_of(jnp.maximum(place - hop, 0) * rows, rows)
        return jnp.where(place >= hop, seg_ref[:, pl.ds(at, rows)], -1)

    seg_q = segments(0)
    for block, hop in enumerate(range(before, -1, -1)):
        allowed = as_column(segments(hop)) == seg_q
        if hop == 0:
            allowed = allowed & (iota((rows, rows), 0) <= iota((rows, rows), 1))
        bias_ref[block * rows : (block + 1) * rows, :] = jnp.where(allowed, 0.0, -jnp.inf)
    slots = placing_ref.shape[0]
    ids_row = ids_ref[...]
    token_slots = slots_of(ids_row, splits, capacity, 1)
    placing_ref[...] = one_hot(token_slots, iota((slots, rows), 0))
    token_slots = slots_of(ids_row, splits, capacity, 0)
    picking_ref[...] = one_hot(token_slots, iota((rows, slots), 1))
    gates_ref[...] = jnp.broadcast_to(as_column(gate_row_ref[...]), gates_ref.shape)
    for copy in copies[3:]:
        copy.wait()


def stage(before, splits, capacity, slots, seg, ids, gates, *large):
    rows = large[0].shape[0]
    sources = (seg, ids, gates, *large)
    return pl.pallas_call(
        functools.partial(stage_kernel, before, splits, capacity),
        out_shape=(
            *[pltpu.VMEM(array.shape, array.dtype) for array in large],
            pltpu.VMEM(((before + 1) * rows, rows), F32),
            pltpu.VMEM((slots, rows), BF16),
            pltpu.VMEM((rows, slots), BF16),
            pltpu.VMEM((rows, rows), F32),
        ),
        in_specs=[HBM] * len(sources),
        out_specs=(VMEM,) * (len(large) + 4),
        scratch_shapes=[
            *[pltpu.VMEM(array.shape, array.dtype) for array in (seg, ids, gates)],
            pltpu.SemaphoreType.DMA((32,)),
        ],
        compiler_params=pltpu.CompilerParams(vmem_limit_bytes=16 * MIB),
        cost_estimate=pl.CostEstimate(flops=0, bytes_accessed=10 * MIB, transcendentals=0),
        name="stage",
    )(*[pltpu.with_memory_space_constraint(array, pltpu.HBM) for array in sources])


def place_of(device, seq_count):
    low = device & (seq_count - 1)
    return device - low + ((seq_count - low) & (seq_count - 1))


def slots_of(ids_row, splits, capacity, axis):
    count = ids_row.shape[1]
    ids_col = as_column(ids_row)
    earlier = iota((count, count), 1 - axis) < iota((count, count), axis)
    same = ((ids_col == ids_row) & earlier).astype(F32)
    rank = jnp.sum(same, axis=1 - axis, keepdims=True).astype(jnp.int32)
    first = (ids_row if axis == 1 else ids_col) * splits
    seq_count = lax.axis_size("seq")
    return [place_of(first + split, seq_count) * capacity + rank for split in range(splits)]


def one_hot(slots, slot_at):
    hot = slot_at == slots[0]
    for slot in slots[1:]:
        hot = hot | (slot_at == slot)
    return hot.astype(F32).astype(BF16)


def weigh_kernel(blocks, *refs):
    key_refs, (q_ref, bias_ref, weight_ref, totals_ref, score_ref) = refs[:blocks], refs[blocks:]
    bias = jnp.concatenate([bias_ref[...]] * 2, 1)
    head_keys = [
        jnp.concatenate([ref[:, head_cols(kv_head)] for ref in key_refs], 0)
        for kv_head in range(KVH)
    ]
    for pair in range(PAIRS):
        pair_queries = jnp.concatenate([q_ref[:, head_cols(2 * pair + i)] for i in range(2)], 0)
        products = lax.dot_general(
            head_keys[2 * pair // GROUP], pair_queries, BY_ROWS, preferred_element_type=F32
        )
        score_ref[pair] = products * SCALE + bias
    for pair in range(PAIRS):
        scores = score_ref[pair]
        weights = jnp.exp(scores - jnp.max(scores, axis=0, keepdims=True))
        totals_ref[pair : pair + 1, :] = jnp.sum(weights, axis=0, keepdims=True)
        weight_ref[pair] = weights.astype(BF16)


def weigh(keys, queries, bias):
    rows = queries.shape[0]
    shape = (PAIRS, len(keys) * rows, 2 * rows)
    operands = (*keys, queries, bias)
    return pl.pallas_call(
        functools.partial(weigh_kernel, len(keys)),
        out_shape=(pltpu.VMEM(shape, BF16), pltpu.VMEM((PAIRS, 2 * rows), F32)),
        in_specs=[VMEM] * len(operands),
        out_specs=(VMEM, VMEM),
        scratch_shapes=[pltpu.VMEM(shape, F32)],
        compiler_params=pltpu.CompilerParams(vmem_limit_bytes=24 * MIB),
        cost_estimate=pl.CostEstimate(
            flops=4 * len(keys) * rows * rows * HEADS * HD, bytes_accessed=MIB, transcendentals=0
        ),
        name="weigh",
    )(*operands)


def mix_kernel(blocks, *refs):
    value_refs, refs = refs[:blocks], refs[blocks:]
    weight_ref, totals_ref, resid_ref, gain_ref, placing_ref = refs[:5]
    hidden_ref, outgoing_ref, turn_ref = refs[5:]
    rows = resid_ref.shape[0]
    eye = (iota((rows, rows), 0) == iota((rows, rows), 1)).astype(F32).astype(BF16)

    def turned(block):
        return lax.dot_general(eye, block, BY_ROWS, preferred_element_type=F32)

    values_t = [
        jnp.concatenate(
            [turned(ref[:, head_cols(kv_head)]).astype(BF16) for ref in value_refs], 1
        )
        for kv_head in range(KVH)
    ]
    scale = 1.0 / totals_ref[...]
    for pair in range(PAIRS):
        mixture = jnp.dot(
            values_t[2 * pair // GROUP], weight_ref[pair], preferred_element_type=F32
        )
        attended = (mixture * scale[pair : pair + 1, :]).astype(BF16)
        for i in range(2):
            turn_ref[head_cols(2 * pair + i), :] = attended[:, i * rows : (i + 1) * rows]
    step = 512
    squares = jnp.zeros((rows, HD), F32)
    for low in range(0, HEADS * HD, step):
        cols = slice(low, low + step)
        attended = turned(turn_ref[cols, :])
        hidden = (resid_ref[:, cols].astype(F32) + attended).astype(BF16)
        hidden_ref[:, cols] = hidden
        hidden_float = hidden.astype(F32)
        square = hidden_float * hidden_float
        for at in range(0, step, HD):
            squares += square[:, at : at + HD]
    sumsq = jnp.sum(squares, axis=-1, keepdims=True)
    inverse = jnp.broadcast_to(lax.rsqrt(sumsq / (HEADS * HD) + EPS), (rows, step))
    placing = placing_ref[...]
    for low in range(0, HEADS * HD, step):
        cols = slice(low, low + step)
        normed = (hidden_ref[:, cols].astype(F32) * inverse * gain_ref[:, cols]).astype(BF16)
        outgoing_ref[:, cols] = jnp.dot(placing, normed, preferred_element_type=F32).astype(BF16)


def mix(values, weights, totals, resid, gain, placing):
    rows, model_width = resid.shape
    operands = (*values, weights, totals, resid, gain, placing)
    return pl.pallas_call(
        functools.partial(mix_kernel, len(values)),
        out_shape=(
            pltpu.VMEM((rows, model_width), BF16),
            pltpu.VMEM((placing.shape[0], model_width), BF16),
        ),
        in_specs=[VMEM] * len(operands),
        out_specs=(VMEM, VMEM),
        scratch_shapes=[pltpu.VMEM((model_width, rows), BF16)],
        compiler_params=pltpu.CompilerParams(vmem_limit_bytes=16 * MIB),
        name="mix",
    )(*operands)


def expert_kernel(x_ref, in_ref, down_ref, out_ref, active_ref):
    units = down_ref.shape[1]
    tile = 256
    rows_in = x_ref[...]
    for low in range(0, units, tile):
        gate = jnp.dot(rows_in, in_ref[0, :, low : low + tile], preferred_element_type=F32)
        up_cols = slice(units + low, units + low + tile)
        up = jnp.dot(rows_in, in_ref[0, :, up_cols], preferred_element_type=F32)
        active_ref[:, low : low + tile] = (gate / (1.0 + jnp.exp(-gate)) * up).astype(BF16)
    active = active_ref[...]
    step = 512
    for low in range(0, out_ref.shape[1], step):
        cols = slice(low, low + step)
        out_ref[:, cols] = jnp.dot(
            active, down_ref[0, :, cols], preferred_element_type=F32
        ).astype(BF16)


def experts(rows_in, w_in, w_out):
    rows, model_width = rows_in.shape
    units = w_out.shape[1]
    if units % 256:
        gate_up = jnp.dot(rows_in, w_in[0], preferred_element_type=F32)
        active = (jax.nn.silu(gate_up[:, :units]) * gate_up[:, units:]).astype(BF16)
        return jnp.dot(active, w_out[0], preferred_element_type=F32).astype(BF16)
    return pl.pallas_call(
        expert_kernel,
        out_shape=jax.ShapeDtypeStruct((rows, model_width), BF16),
        in_specs=[VMEM] * 3,
        out_specs=VMEM,
        scratch_shapes=[pltpu.VMEM((rows, units), BF16)],
        compiler_params=pltpu.CompilerParams(vmem_limit_bytes=16 * MIB),
        name="experts",
    )(rows_in, w_in, w_out)


def combine_kernel(delivered_ref, hidden_ref, picking_ref, gates_ref, out_ref, made_ref, sems):
    step = 512
    gates = jnp.concatenate([gates_ref[...]] * (step // gates_ref.shape[1]), 1)
    picking = picking_ref[...]
    copies = []
    for low in range(0, hidden_ref.shape[1], step):
        cols = slice(low, low + step)
        routed = jnp.dot(picking, delivered_ref[:, cols], preferred_element_type=F32)
        routed = routed.astype(BF16).astype(F32)
        made_ref[:, cols] = (hidden_ref[:, cols].astype(F32) + gates * routed).astype(BF16)
        copies.append(
            pltpu.make_async_copy(made_ref.at[:, cols], out_ref.at[:, cols], sems.at[low // step])
        )
        copies[-1].start()
    for copy in copies:
        copy.wait()


def combine(delivered, hidden, picking, gates):
    return pl.pallas_call(
        combine_kernel,
        out_shape=pltpu.HBM(hidden.shape, BF16),
        in_specs=[VMEM] * 4,
        out_specs=HBM,
        scratch_shapes=[
            pltpu.VMEM(hidden.shape, BF16),
            pltpu.SemaphoreType.DMA((hidden.shape[1] // 512,)),
        ],
        compiler_params=pltpu.CompilerParams(vmem_limit_bytes=16 * MIB),
        name="combine",
    )(delivered, hidden, picking, gates)


def per_device(
    queries, keys, values, resid, seg_ids, norm_gain, expert_ids, gate_weights, w_in, w_out
):
    seq_count = lax.axis_size("seq")
    exp_count = lax.axis_size("exp")
    devices = seq_count * exp_count
    rows, model_width = resid.shape
    length = rows * seq_count
    splits = FF // w_out.shape[1]
    capacity = max(2, 2 * rows * splits // devices)
    slots = devices * capacity
    reach = length // 2
    before = min(seq_count - 1, -(-(reach - 1) // rows))


    def earlier(own):
        return [
            lax.ppermute(own, "seq", [(i, (i + hop) % seq_count if i + hop < seq_count else (seq_count - 1 - i) if hop == 2 else (i + hop) % seq_count) for i in range(seq_count)])
            for hop in range(before, 0, -1)
        ]

    key_blocks, value_blocks = earlier(keys), earlier(values)
    queries, keys, values, resid, gain, w_in, bias, placing, picking, gates = stage(
        before, splits, capacity, slots, seg_ids[None], expert_ids[None], gate_weights[None],
        queries, keys, values, resid, norm_gain[None], w_in,
    )
    weights, totals = weigh([*key_blocks, keys], queries, bias)
    hidden, outgoing = mix([*value_blocks, values], weights, totals, resid, gain, placing)

    def exchange(block):
        return lax.all_to_all(
            block.reshape(devices, capacity, model_width),
            ("exp", "seq"),
            split_axis=0,
            concat_axis=0,
            tiled=True,
            axis_index_groups=[[place_of(device, seq_count) for device in range(devices)]],
        ).reshape(slots, model_width)

    delivered = exchange(experts(exchange(outgoing), w_in, w_out))
    return combine(delivered, hidden, picking, gates)


def solution(mesh):
    placed = (
        P(("exp", "seq"), None),
        P(("exp", "seq"), None),
        P(("exp", "seq"), None),
        P(("exp", "seq"), None),
        P("exp"),
        P(),
        P(("exp", "seq")),
        P(("exp", "seq")),
        P(("exp", "seq"), None, None),
        P(("exp", "seq"), None, None),
    )
    return jax.shard_map(
        per_device, mesh=mesh, in_specs=placed, out_specs=P(("exp", "seq"), None), check_vma=False
    )
```

```python
import functools
import math

import jax
import jax.numpy as jnp
from jax import lax
from jax.experimental import pallas as pl
from jax.experimental.pallas import tpu as pltpu
from jax.sharding import PartitionSpec as P

HD = 128
HEADS = 16
KVH = 2
EXP_DEV = 4
FF = 768
EPS = 1e-6
F32 = jnp.float32
BF16 = jnp.bfloat16
VMEM = pl.BlockSpec(memory_space=pltpu.VMEM)
HBM = pl.BlockSpec(memory_space=pltpu.HBM)
SCALE = 1.0 / math.sqrt(HD)
GROUP = HEADS // KVH
MIB = 2**20
STAGED = 9
PAIRS = HEADS // 2
BY_ROWS = (((1,), (1,)), ((), ()))


def head_cols(head):
    return slice(head * HD, (head + 1) * HD)


def iota(shape, dimension):
    return lax.broadcasted_iota(jnp.int32, shape, dimension)


def as_column(row):
    count = row.shape[1]
    square = jnp.broadcast_to(row, (count, count))
    eye = iota((count, count), 0) == iota((count, count), 1)
    kept = jnp.where(eye, square, jnp.zeros_like(square))
    if row.dtype == jnp.int32:
        return jnp.sum(kept.astype(F32), axis=1, keepdims=True).astype(jnp.int32)
    return jnp.sum(kept, axis=1, keepdims=True)


def pieces(source, target):
    axis, count = source.ndim - 2, source.shape[-2]
    parts = max(1, source.size // MIB)
    while count % (16 * parts):
        parts -= 1
    step = count // parts
    for low in range(0, count, step):
        at = (0,) * axis + (slice(low, low + step),)
        yield source.at[at], target.at[at]


def stage_kernel(before, splits, capacity, *refs):
    count = STAGED
    sources, refs = refs[:count], refs[count:]
    copied, refs = refs[: count - 3], refs[count - 3 :]
    bias_ref, placing_ref, picking_ref, gates_ref, refs = *refs[:4], refs[4:]
    small, sems = refs[:3], refs[3]
    copies = []
    for source, target in zip(sources, (*small, *copied)):
        whole = source.shape[-2] % 16 != 0
        for part, place_for in [(source, target)] if whole else pieces(source, target):
            copies.append(pltpu.make_async_copy(part, place_for, sems.at[len(copies)]))
    for copy in copies:
        copy.start()
    seg_ref, ids_ref, gate_row_ref = small
    for copy in copies[:3]:
        copy.wait()
    rows = bias_ref.shape[1]
    place = lax.axis_index("seq")

    def segments(hop):
        at = pl.multiple_of(jnp.maximum(place - hop, 0) * rows, rows)
        return jnp.where(place >= hop, seg_ref[:, pl.ds(at, rows)], -1)

    seg_q = segments(0)
    for block, hop in enumerate(range(before, -1, -1)):
        allowed = as_column(segments(hop)) == seg_q
        if hop == 0:
            allowed = allowed & (iota((rows, rows), 0) <= iota((rows, rows), 1))
        bias_ref[block * rows : (block + 1) * rows, :] = jnp.where(allowed, 0.0, -jnp.inf)
    slots = placing_ref.shape[0]
    ids_row = ids_ref[...]
    token_slots = slots_of(ids_row, splits, capacity, 1)
    placing_ref[...] = one_hot(token_slots, iota((slots, rows), 0))
    token_slots = slots_of(ids_row, splits, capacity, 0)
    picking_ref[...] = one_hot(token_slots, iota((rows, slots), 1))
    gates_ref[...] = jnp.broadcast_to(as_column(gate_row_ref[...]), gates_ref.shape)
    for copy in copies[3:]:
        copy.wait()


def stage(before, splits, capacity, slots, seg, ids, gates, *large):
    rows = large[0].shape[0]
    sources = (seg, ids, gates, *large)
    return pl.pallas_call(
        functools.partial(stage_kernel, before, splits, capacity),
        out_shape=(
            *[pltpu.VMEM(array.shape, array.dtype) for array in large],
            pltpu.VMEM(((before + 1) * rows, rows), F32),
            pltpu.VMEM((slots, rows), BF16),
            pltpu.VMEM((rows, slots), BF16),
            pltpu.VMEM((rows, rows), F32),
        ),
        in_specs=[HBM] * len(sources),
        out_specs=(VMEM,) * (len(large) + 4),
        scratch_shapes=[
            *[pltpu.VMEM(array.shape, array.dtype) for array in (seg, ids, gates)],
            pltpu.SemaphoreType.DMA((32,)),
        ],
        compiler_params=pltpu.CompilerParams(vmem_limit_bytes=16 * MIB),
        cost_estimate=pl.CostEstimate(flops=0, bytes_accessed=10 * MIB, transcendentals=0),
        name="stage",
    )(*[pltpu.with_memory_space_constraint(array, pltpu.HBM) for array in sources])


def place_of(device, seq_count, exp_count):
    low = device & (seq_count - 1)
    index = (device - low) // seq_count
    core, chip = index & 1, index >> 1
    high, odd = (chip >> 1) & 1, chip & 1
    index = exp_count - 1 - (((chip >> 2) << 3) | ((high ^ odd) << 2) | (high << 1) | core)
    return index * seq_count + ((seq_count - low) & (seq_count - 1))


def slots_of(ids_row, splits, capacity, axis):
    count = ids_row.shape[1]
    ids_col = as_column(ids_row)
    earlier = iota((count, count), 1 - axis) < iota((count, count), axis)
    same = ((ids_col == ids_row) & earlier).astype(F32)
    rank = jnp.sum(same, axis=1 - axis, keepdims=True).astype(jnp.int32)
    first = (ids_row if axis == 1 else ids_col) * splits
    seq_count = lax.axis_size("seq")
    exp_count = lax.axis_size("exp")
    return [
        place_of(first + split, seq_count, exp_count) * capacity + rank for split in range(splits)
    ]


def one_hot(slots, slot_at):
    hot = slot_at == slots[0]
    for slot in slots[1:]:
        hot = hot | (slot_at == slot)
    return hot.astype(F32).astype(BF16)


def weigh_kernel(blocks, *refs):
    key_refs, (q_ref, bias_ref, weight_ref, totals_ref, score_ref) = refs[:blocks], refs[blocks:]
    bias = jnp.concatenate([bias_ref[...]] * 2, 1)
    head_keys = [
        jnp.concatenate([ref[:, head_cols(kv_head)] for ref in key_refs], 0)
        for kv_head in range(KVH)
    ]
    for pair in range(PAIRS):
        pair_queries = jnp.concatenate([q_ref[:, head_cols(2 * pair + i)] for i in range(2)], 0)
        products = lax.dot_general(
            head_keys[2 * pair // GROUP], pair_queries, BY_ROWS, preferred_element_type=F32
        )
        score_ref[pair] = products * SCALE + bias
    for pair in range(PAIRS):
        scores = score_ref[pair]
        weights = jnp.exp(scores - jnp.max(scores, axis=0, keepdims=True))
        totals_ref[pair : pair + 1, :] = jnp.sum(weights, axis=0, keepdims=True)
        weight_ref[pair] = weights.astype(BF16)


def weigh(keys, queries, bias):
    rows = queries.shape[0]
    shape = (PAIRS, len(keys) * rows, 2 * rows)
    operands = (*keys, queries, bias)
    return pl.pallas_call(
        functools.partial(weigh_kernel, len(keys)),
        out_shape=(pltpu.VMEM(shape, BF16), pltpu.VMEM((PAIRS, 2 * rows), F32)),
        in_specs=[VMEM] * len(operands),
        out_specs=(VMEM, VMEM),
        scratch_shapes=[pltpu.VMEM(shape, F32)],
        compiler_params=pltpu.CompilerParams(vmem_limit_bytes=24 * MIB),
        cost_estimate=pl.CostEstimate(
            flops=4 * len(keys) * rows * rows * HEADS * HD, bytes_accessed=MIB, transcendentals=0
        ),
        name="weigh",
    )(*operands)


def mix_kernel(blocks, *refs):
    value_refs, refs = refs[:blocks], refs[blocks:]
    weight_ref, totals_ref, resid_ref, gain_ref, placing_ref = refs[:5]
    hidden_ref, outgoing_ref, turn_ref = refs[5:]
    rows = resid_ref.shape[0]
    eye = (iota((rows, rows), 0) == iota((rows, rows), 1)).astype(F32).astype(BF16)

    def turned(block):
        return lax.dot_general(eye, block, BY_ROWS, preferred_element_type=F32)

    values_t = [
        jnp.concatenate(
            [turned(ref[:, head_cols(kv_head)]).astype(BF16) for ref in value_refs], 1
        )
        for kv_head in range(KVH)
    ]
    scale = 1.0 / totals_ref[...]
    for pair in range(PAIRS):
        mixture = jnp.dot(
            values_t[2 * pair // GROUP], weight_ref[pair], preferred_element_type=F32
        )
        attended = (mixture * scale[pair : pair + 1, :]).astype(BF16)
        for i in range(2):
            turn_ref[head_cols(2 * pair + i), :] = attended[:, i * rows : (i + 1) * rows]
    step = 512
    squares = jnp.zeros((rows, HD), F32)
    for low in range(0, HEADS * HD, step):
        cols = slice(low, low + step)
        attended = turned(turn_ref[cols, :])
        hidden = (resid_ref[:, cols].astype(F32) + attended).astype(BF16)
        hidden_ref[:, cols] = hidden
        hidden_float = hidden.astype(F32)
        square = hidden_float * hidden_float
        for at in range(0, step, HD):
            squares += square[:, at : at + HD]
    sumsq = jnp.sum(squares, axis=-1, keepdims=True)
    inverse = jnp.broadcast_to(lax.rsqrt(sumsq / (HEADS * HD) + EPS), (rows, step))
    placing = placing_ref[...]
    for low in range(0, HEADS * HD, step):
        cols = slice(low, low + step)
        normed = (hidden_ref[:, cols].astype(F32) * inverse * gain_ref[:, cols]).astype(BF16)
        outgoing_ref[:, cols] = jnp.dot(placing, normed, preferred_element_type=F32).astype(BF16)


def mix(values, weights, totals, resid, gain, placing):
    rows, model_width = resid.shape
    operands = (*values, weights, totals, resid, gain, placing)
    return pl.pallas_call(
        functools.partial(mix_kernel, len(values)),
        out_shape=(
            pltpu.VMEM((rows, model_width), BF16),
            pltpu.VMEM((placing.shape[0], model_width), BF16),
        ),
        in_specs=[VMEM] * len(operands),
        out_specs=(VMEM, VMEM),
        scratch_shapes=[pltpu.VMEM((model_width, rows), BF16)],
        compiler_params=pltpu.CompilerParams(vmem_limit_bytes=16 * MIB),
        name="mix",
    )(*operands)


def expert_kernel(x_ref, in_ref, down_ref, out_ref, active_ref):
    units = down_ref.shape[1]
    tile = 256
    rows_in = x_ref[...]
    for low in range(0, units, tile):
        gate = jnp.dot(rows_in, in_ref[0, :, low : low + tile], preferred_element_type=F32)
        up_cols = slice(units + low, units + low + tile)
        up = jnp.dot(rows_in, in_ref[0, :, up_cols], preferred_element_type=F32)
        active_ref[:, low : low + tile] = (gate / (1.0 + jnp.exp(-gate)) * up).astype(BF16)
    active = active_ref[...]
    step = 512
    for low in range(0, out_ref.shape[1], step):
        cols = slice(low, low + step)
        out_ref[:, cols] = jnp.dot(
            active, down_ref[0, :, cols], preferred_element_type=F32
        ).astype(BF16)


def experts(rows_in, w_in, w_out):
    rows, model_width = rows_in.shape
    units = w_out.shape[1]
    if units % 256:
        gate_up = jnp.dot(rows_in, w_in[0], preferred_element_type=F32)
        active = (jax.nn.silu(gate_up[:, :units]) * gate_up[:, units:]).astype(BF16)
        return jnp.dot(active, w_out[0], preferred_element_type=F32).astype(BF16)
    return pl.pallas_call(
        expert_kernel,
        out_shape=jax.ShapeDtypeStruct((rows, model_width), BF16),
        in_specs=[VMEM] * 3,
        out_specs=VMEM,
        scratch_shapes=[pltpu.VMEM((rows, units), BF16)],
        compiler_params=pltpu.CompilerParams(vmem_limit_bytes=16 * MIB),
        name="experts",
    )(rows_in, w_in, w_out)


def combine_kernel(delivered_ref, hidden_ref, picking_ref, gates_ref, out_ref, made_ref, sems):
    step = 512
    gates = jnp.concatenate([gates_ref[...]] * (step // gates_ref.shape[1]), 1)
    picking = picking_ref[...]
    copies = []
    for low in range(0, hidden_ref.shape[1], step):
        cols = slice(low, low + step)
        routed = jnp.dot(picking, delivered_ref[:, cols], preferred_element_type=F32)
        routed = routed.astype(BF16).astype(F32)
        made_ref[:, cols] = (hidden_ref[:, cols].astype(F32) + gates * routed).astype(BF16)
        copies.append(
            pltpu.make_async_copy(made_ref.at[:, cols], out_ref.at[:, cols], sems.at[low // step])
        )
        copies[-1].start()
    for copy in copies:
        copy.wait()


def combine(delivered, hidden, picking, gates):
    return pl.pallas_call(
        combine_kernel,
        out_shape=pltpu.HBM(hidden.shape, BF16),
        in_specs=[VMEM] * 4,
        out_specs=HBM,
        scratch_shapes=[
            pltpu.VMEM(hidden.shape, BF16),
            pltpu.SemaphoreType.DMA((hidden.shape[1] // 512,)),
        ],
        compiler_params=pltpu.CompilerParams(vmem_limit_bytes=16 * MIB),
        name="combine",
    )(delivered, hidden, picking, gates)


def per_device(
    queries, keys, values, resid, seg_ids, norm_gain, expert_ids, gate_weights, w_in, w_out
):
    seq_count = lax.axis_size("seq")
    exp_count = lax.axis_size("exp")
    devices = seq_count * exp_count
    rows, model_width = resid.shape
    length = rows * seq_count
    splits = FF // w_out.shape[1]
    capacity = max(2, 2 * rows * splits // devices)
    slots = devices * capacity
    reach = length // 2
    before = min(seq_count - 1, -(-(reach - 1) // rows))


    def earlier(own):
        return [
            lax.ppermute(own, "seq", [(i, (i + hop) % seq_count if i + hop < seq_count else (seq_count - 1 - i) if hop == 2 else (i + hop) % seq_count) for i in range(seq_count)])
            for hop in range(before, 0, -1)
        ]

    key_blocks, value_blocks = earlier(keys), earlier(values)
    queries, keys, values, resid, gain, w_in, bias, placing, picking, gates = stage(
        before, splits, capacity, slots, seg_ids[None], expert_ids[None], gate_weights[None],
        queries, keys, values, resid, norm_gain[None], w_in,
    )
    weights, totals = weigh([*key_blocks, keys], queries, bias)
    hidden, outgoing = mix([*value_blocks, values], weights, totals, resid, gain, placing)

    order = sorted(range(devices), key=lambda device: place_of(device, seq_count, exp_count))

    def exchange(block):
        return lax.all_to_all(
            block.reshape(devices, capacity, model_width),
            ("exp", "seq"),
            split_axis=0,
            concat_axis=0,
            tiled=True,
            axis_index_groups=[order],
        ).reshape(slots, model_width)

    delivered = exchange(experts(exchange(outgoing), w_in, w_out))
    return combine(delivered, hidden, picking, gates)


def solution(mesh):
    placed = (
        P(("exp", "seq"), None),
        P(("exp", "seq"), None),
        P(("exp", "seq"), None),
        P(("exp", "seq"), None),
        P("exp"),
        P(),
        P(("exp", "seq")),
        P(("exp", "seq")),
        P(("exp", "seq"), None, None),
        P(("exp", "seq"), None, None),
    )
    return jax.shard_map(
        per_device, mesh=mesh, in_specs=placed, out_specs=P(("exp", "seq"), None), check_vma=False
    )
```
